32 devices in a mesh: groups: 2 (over y), pr: 4 (over z), pc: 4 (over x, core).
Axes of the slice: x: 2, y: 2, z: 4, core: 2. Of those that a mesh axis runs over, the one named last changes fastest.
Arguments:
- matrix: float32 [2, 2048, 1, 2048], P('groups', 'pr', None, 'pc'), parts along dimension 0, as said below
Outputs:
- factored: float32 [2, 2048, 1, 2048], P('groups', 'pr', None, 'pc'), parts along dimension 0
There are 2 independent parts, one for each index of `groups`. The reference program is written for one: setup_inputs(seed, part) draws one part's arguments, and reference() takes and returns one part's arrays. A program takes and returns all parts, laid end to end along the dimension named above; each array names one. Nothing has to cross between parts.
Inputs may be any that keep to these rules, and one draw needn't show every extreme that they name: The symmetric matrix given by the lower triangle of matrix is positive definite.
All inputs are finite; a program needn't handle non-finite values.
Results may differ from the reference program's by a relative error of at most 0.0001.
Values sent between devices are 32-bit elements; how exact they have to be, the bound alone decides.
A program may use at most 64 MiB of HBM per device.

```python
import math
import jax
import jax.numpy as jnp
from jax import lax

NB = 512
RC = 1
CC = 1
N_PR = 4
N_PC = 4


def draw_matrix(key, part):
    key = jax.random.fold_in(key, 11)
    shape = (RC, N_PR * NB, CC, N_PC * NB)
    order = RC * N_PR * NB
    key_values = jax.random.fold_in(key, 1)
    key_scales = jax.random.fold_in(key, 2)
    jitter = jax.random.normal(key_values, shape, jnp.float32)
    scales = jax.random.uniform(key_scales, (order,), jnp.float32, 0.6, 1.4)
    near_length = NB / 8.0
    far_weight = 0.15
    diagonal_lift = 1.0
    rows = lax.broadcasted_iota(jnp.int32, shape, 0) * (N_PR * NB) + lax.broadcasted_iota(jnp.int32, shape, 1)
    cols = lax.broadcasted_iota(jnp.int32, shape, 2) * (N_PC * NB) + lax.broadcasted_iota(jnp.int32, shape, 3)
    distance = jnp.abs(rows - cols).astype(jnp.float32)
    row_scale = scales.reshape(RC, N_PR * NB, 1, 1)
    col_scale = scales.reshape(1, 1, CC, N_PC * NB)
    kernel = jnp.exp(-distance / near_length) + far_weight * jnp.exp(-distance * (2.0 / order))
    values = row_scale * col_scale * kernel + 0.2 / math.sqrt(order) * jitter
    return jnp.where(rows == cols, values + diagonal_lift, values)


def setup_inputs(seed: int = 0, part: int = 0) -> dict:
    keys = jax.random.split(jax.random.key(seed), 2)
    part_splits = jax.random.split(jax.random.fold_in(keys[1], part), 2)
    matrix = draw_matrix(jax.random.fold_in(jax.random.fold_in(keys[1], part), 71), part)
    return {"matrix": matrix}


def symmetric(block):
    return jnp.tril(block) + jnp.tril(block, -1).T

def reference(matrix):
    order = RC * N_PR * NB
    full = matrix.reshape(order, order)
    tile_of = jnp.arange(order, dtype=jnp.int32) // NB
    for step in range(2):
        start = step * NB
        finish = start + NB
        factor = jnp.linalg.cholesky(symmetric(full[start:finish, start:finish]))
        panel = lax.linalg.triangular_solve(factor, full[finish:, start:finish], left_side=False, lower=True, transpose_a=True)
        product = jnp.dot(panel.astype(jnp.float32), panel.T.astype(jnp.float32), precision=lax.Precision.HIGHEST, preferred_element_type=jnp.float32)
        keep = tile_of[finish:, None] >= tile_of[None, finish:]
        full = full.at[start:finish, start:finish].set(factor)
        full = full.at[finish:, start:finish].set(panel)
        full = full.at[finish:, finish:].add(jnp.where(keep, -product, jnp.float32(0.0)))
    return full.reshape(matrix.shape)
```

```python
import functools

import jax
import jax.numpy as jnp
from jax import lax
from jax.experimental import pallas as pl
from jax.experimental.pallas import tpu as pltpu
from jax.sharding import PartitionSpec as P

BLK = 128
G = 8


def nt(a, b):
    return lax.dot_general(
        a, b, (((1,), (1,)), ((), ())),
        precision=lax.Precision.HIGHEST, preferred_element_type=jnp.float32,
    )


def factor_block(a):
    n = BLK
    ng = n // G
    sub = lax.broadcasted_iota(jnp.int32, (G, n), 0)
    lane = lax.broadcasted_iota(jnp.int32, (G, n), 1)
    left = [a[g * G:(g + 1) * G, :] for g in range(ng)]
    right = [jnp.where(lane == sub + g * G, 1.0, 0.0).astype(jnp.float32) for g in range(ng)]
    for g in range(ng):
        own_l, own_r = left[g], right[g]
        lo = g * G
        nxt = g + 1 < ng
        own_c = [jnp.broadcast_to(own_l[:, lo + j:lo + j + 1], (G, n)) for j in range(G)]
        if nxt:
            nx_l, nx_r = left[g + 1], right[g + 1]
            nx_c = [jnp.broadcast_to(nx_l[:, lo + j:lo + j + 1], (G, n)) for j in range(G)]
        rows_l, rows_r = [], []
        for j in range(G):
            q = lax.rsqrt(jnp.broadcast_to(own_c[j][j:j + 1, :], (G, n)))
            row_l = jnp.broadcast_to(own_l[j:j + 1, :], (G, n)) * q
            row_r = jnp.broadcast_to(own_r[j:j + 1, :], (G, n)) * q
            rows_l.append(row_l)
            rows_r.append(row_r)
            mult = own_c[j] * q
            heads = [jnp.broadcast_to(own_c[t][j:j + 1, :], (G, n)) * q for t in range(j + 1, G)]
            for t in range(j + 1, G):
                own_c[t] = own_c[t] - mult * heads[t - j - 1]
            own_l = own_l - mult * row_l
            own_r = own_r - mult * row_r
            if nxt:
                mult = nx_c[j] * q
                for t in range(j + 1, G):
                    nx_c[t] = nx_c[t] - mult * heads[t - j - 1]
                nx_l = nx_l - mult * row_l
                nx_r = nx_r - mult * row_r
        fin_l, fin_r = rows_l[0], rows_r[0]
        for j in range(1, G):
            fin_l = jnp.where(sub == j, rows_l[j], fin_l)
            fin_r = jnp.where(sub == j, rows_r[j], fin_r)
        left[g], right[g] = fin_l, fin_r
        if nxt:
            left[g + 1], right[g + 1] = nx_l, nx_r
        if g + 2 < ng:
            turned = fin_l.T
            for h in range(g + 2, ng):
                tl, tr = left[h], right[h]
                for j in range(G):
                    m = jnp.broadcast_to(turned[h * G:(h + 1) * G, j:j + 1], (G, n))
                    tl = tl - m * rows_l[j]
                    tr = tr - m * rows_r[j]
                left[h], right[h] = tl, tr
    lt = jnp.concatenate(left, 0)
    w = jnp.concatenate(right, 0)
    return lt, w

def kernel(n_r, n_c, n_cc, nb, x_ref, o_ref, work, diag, fbuf, panels,
           f_send, f_recv, p_send, p_recv):
    parts = nb // BLK
    r = lax.axis_index("pr")
    c = lax.axis_index("pc")
    near = lax.rem(c + 1, n_c)

    barrier = pltpu.get_barrier_semaphore()

    def greet(i, _):
        @pl.when(i != r * n_c + c)
        def _():
            pl.semaphore_signal(
                barrier, inc=1, device_id={"pr": i // n_c, "pc": lax.rem(i, n_c)},
                device_id_type=pl.DeviceIdType.MESH)
        return 0

    lax.fori_loop(0, n_r * n_c, greet, 0)
    o_ref[...] = x_ref[...]

    @pl.when(c < 2)
    def _():
        for m in range(parts):
            work[m] = x_ref[0, :, m * BLK:(m + 1) * BLK]

    pl.semaphore_wait(barrier, n_r * n_c - 1)

    def factor_copy(k, m, to):
        ref = fbuf.at[k, m, pl.ds(m * BLK, nb - m * BLK), :]
        return pltpu.make_async_remote_copy(
            src_ref=ref, dst_ref=ref, send_sem=f_send.at[k, m, to], recv_sem=f_recv.at[k, m],
            device_id={"pr": to}, device_id_type=pl.DeviceIdType.MESH)

    def row_copy(k, m, to):
        ref = panels.at[k, 0, m]
        return pltpu.make_async_remote_copy(
            src_ref=ref, dst_ref=ref, send_sem=p_send.at[k, m, to], recv_sem=p_recv.at[k, 0, m],
            device_id={"pc": to}, device_id_type=pl.DeviceIdType.MESH)

    def col_copy(k, m, to):
        slot = 1 + r // n_c
        return pltpu.make_async_remote_copy(
            src_ref=panels.at[k, 0, m], dst_ref=panels.at[k, slot, m],
            send_sem=p_send.at[k, m, n_c + to], recv_sem=p_recv.at[k, slot, m],
            device_id={"pr": to, "pc": lax.rem(r, n_c)}, device_id_type=pl.DeviceIdType.MESH)

    def holds(k, row, col):
        found = (col > k) & (col <= row)
        for b in range(1, n_cc):
            found = found | ((b * n_c + col > k) & (b * n_c + col <= row))
        return found

    def each_row_copy(k, m, act):
        def one(to, _):
            @pl.when((to != k) & holds(k, r, to))
            def _():
                act(row_copy(k, m, to))
            return 0
        lax.fori_loop(0, n_c, one, 0)

    def each_col_copy(k, m, act):
        def one(to, _):
            act(col_copy(k, m, to))
            return 0
        lax.fori_loop(r + 1, n_r, one, 0)

    def each_factor_copy(k, m, act):
        def one(to, _):
            act(factor_copy(k, m, to))
            return 0
        lax.fori_loop(k + 1, n_r, one, 0)

    def step(k, _):
        is_factor = (r == k) & (c == k)
        is_solver = (c == k) & (r > k)

        @pl.when(is_factor)
        def _():
            i0 = lax.broadcasted_iota(jnp.int32, (BLK, BLK), 0)
            i1 = lax.broadcasted_iota(jnp.int32, (BLK, BLK), 1)

            def stage(m, _):
                rows = pl.ds(pl.multiple_of(m * BLK, BLK), BLK)
                low = jnp.where(i0 >= i1, work[m, rows, :], 0.0)
                lt, w = factor_block(jnp.where(i0 >= i1, low, low.T))
                fbuf[k, m, rows, :] = w
                diag[m] = lt
                for mm in range(parts):
                    @pl.when(m == mm)
                    def _():
                        s = (mm + 1) * BLK
                        if s < nb:
                            fbuf[k, mm, s:, :] = nt(work[mm, s:, :], w)
                        each_factor_copy(k, mm, lambda d: d.start())
                        for n in range(mm + 1, parts):
                            t = n * BLK
                            work[n, t:, :] -= nt(fbuf[k, mm, t:, :], fbuf[k, mm, t:t + BLK, :])
                return 0

            lax.fori_loop(0, parts, stage, 0)
            for m in range(parts):
                s, e = m * BLK, (m + 1) * BLK
                if m:
                    o_ref[0, :s, s:e] = jnp.zeros((s, BLK), jnp.float32)
                o_ref[0, s:e, s:e] = jnp.where(i0 <= i1, diag[m], 0.0).T
                if e < nb:
                    o_ref[0, e:, s:e] = fbuf[k, m, e:, :]
            for m in range(parts):
                each_factor_copy(k, m, lambda d: d.wait_send())

        @pl.when(is_solver)
        def _():
            for m in range(parts):
                s, e = m * BLK, (m + 1) * BLK
                factor_copy(k, m, 0).wait_recv()
                part = nt(work[m], fbuf[k, m, s:e, :])
                panels[k, 0, m] = part
                each_row_copy(k, m, lambda d: d.start())
                each_col_copy(k, m, lambda d: d.start())
                o_ref[0, :, s:e] = part
                for n in range(m + 1, parts):
                    work[n] -= nt(part, fbuf[k, m, n * BLK:(n + 1) * BLK, :])

        for m in range(parts):
            @pl.when((c != k) & holds(k, r, c))
            def _():
                row_copy(k, m, near).wait_recv()
            for b in range(n_cc):
                j = b * n_c + c

                @pl.when((j > k) & (j < r))
                def _():
                    pltpu.make_async_remote_copy(
                        src_ref=panels.at[k, 0, m], dst_ref=panels.at[k, 1 + b, m],
                        send_sem=p_send.at[k, m, 0], recv_sem=p_recv.at[k, 1 + b, m],
                        device_id={"pc": near}, device_id_type=pl.DeviceIdType.MESH).wait_recv()

                @pl.when((j > k) & (j <= r))
                def _():
                    slot = jnp.where(j == r, 0, 1 + b)
                    o_ref[b] -= nt(panels[k, 0, m], panels[k, slot, m])

        @pl.when((k == 0) & (c == 1))
        def _():
            for m in range(parts):
                work[m] = o_ref[0, :, m * BLK:(m + 1) * BLK]

        @pl.when(is_solver)
        def _():
            for m in range(parts):
                each_row_copy(k, m, lambda d: d.wait_send())
                each_col_copy(k, m, lambda d: d.wait_send())
        return 0

    lax.fori_loop(0, 2, step, 0)


def on_device(n_r, n_c, matrix):
    _, nb, n_cc, _ = matrix.shape
    parts = nb // BLK
    tiles = jnp.transpose(matrix[0], (1, 0, 2))
    sem = pltpu.SemaphoreType.DMA
    out = pl.pallas_call(
        functools.partial(kernel, n_r, n_c, n_cc, nb),
        out_shape=jax.ShapeDtypeStruct(tiles.shape, jnp.float32),
        in_specs=[pl.BlockSpec(memory_space=pltpu.VMEM)],
        out_specs=pl.BlockSpec(memory_space=pltpu.VMEM),
        scratch_shapes=[
            pltpu.VMEM((parts, nb, BLK), jnp.float32),
            pltpu.VMEM((parts, BLK, BLK), jnp.float32),
            pltpu.VMEM((2, parts, nb, BLK), jnp.float32),
            pltpu.VMEM((2, 1 + n_cc, parts, nb, BLK), jnp.float32),
            sem((2, parts, n_r)),
            sem((2, parts)),
            sem((2, parts, n_c + n_r)),
            sem((2, 1 + n_cc, parts)),
        ],
        compiler_params=pltpu.CompilerParams(
            collective_id=0, has_side_effects=True, vmem_limit_bytes=40 * 2**20),
    )(tiles)
    return jnp.transpose(out, (1, 0, 2))[None]


def solution(mesh):
    n_r, n_c = mesh.shape["pr"], mesh.shape["pc"]
    spec = P("groups", "pr", None, "pc")
    return jax.shard_map(
        functools.partial(on_device, n_r, n_c), mesh=mesh, in_specs=(spec,), out_specs=spec,
        check_vma=False)
```

```python
import functools

import jax
import jax.numpy as jnp
from jax import lax
from jax.experimental import pallas as pl
from jax.experimental.pallas import tpu as pltpu
from jax.sharding import PartitionSpec as P

BLK = 128
G = 8


def nt(a, b):
    return lax.dot_general(
        a, b, (((1,), (1,)), ((), ())),
        precision=lax.Precision.HIGHEST, preferred_element_type=jnp.float32,
    )


def factor_block(a):
    n = BLK
    ng = n // G
    sub = lax.broadcasted_iota(jnp.int32, (G, n), 0)
    lane = lax.broadcasted_iota(jnp.int32, (G, n), 1)
    left = [a[g * G:(g + 1) * G, :] for g in range(ng)]
    right = [jnp.where(lane == sub + g * G, 1.0, 0.0).astype(jnp.float32) for g in range(ng)]
    for g in range(ng):
        own_l, own_r = left[g], right[g]
        lo = g * G
        nxt = g + 1 < ng
        own_c = [jnp.broadcast_to(own_l[:, lo + j:lo + j + 1], (G, n)) for j in range(G)]
        if nxt:
            nx_l, nx_r = left[g + 1], right[g + 1]
            nx_c = [jnp.broadcast_to(nx_l[:, lo + j:lo + j + 1], (G, n)) for j in range(G)]
        rows_l, rows_r = [], []
        for j in range(G):
            q = lax.rsqrt(jnp.broadcast_to(own_c[j][j:j + 1, :], (G, n)))
            row_l = jnp.broadcast_to(own_l[j:j + 1, :], (G, n)) * q
            row_r = jnp.broadcast_to(own_r[j:j + 1, :], (G, n)) * q
            rows_l.append(row_l)
            rows_r.append(row_r)
            mult = own_c[j] * q
            heads = [jnp.broadcast_to(own_c[t][j:j + 1, :], (G, n)) * q for t in range(j + 1, G)]
            for t in range(j + 1, G):
                own_c[t] = own_c[t] - mult * heads[t - j - 1]
            own_l = own_l - mult * row_l
            own_r = own_r - mult * row_r
            if nxt:
                mult = nx_c[j] * q
                for t in range(j + 1, G):
                    nx_c[t] = nx_c[t] - mult * heads[t - j - 1]
                nx_l = nx_l - mult * row_l
                nx_r = nx_r - mult * row_r
        fin_l, fin_r = rows_l[0], rows_r[0]
        for j in range(1, G):
            fin_l = jnp.where(sub == j, rows_l[j], fin_l)
            fin_r = jnp.where(sub == j, rows_r[j], fin_r)
        left[g], right[g] = fin_l, fin_r
        if nxt:
            left[g + 1], right[g + 1] = nx_l, nx_r
        if g + 2 < ng:
            turned = fin_l.T
            for h in range(g + 2, ng):
                tl, tr = left[h], right[h]
                for j in range(G):
                    m = jnp.broadcast_to(turned[h * G:(h + 1) * G, j:j + 1], (G, n))
                    tl = tl - m * rows_l[j]
                    tr = tr - m * rows_r[j]
                left[h], right[h] = tl, tr
    lt = jnp.concatenate(left, 0)
    w = jnp.concatenate(right, 0)
    return lt, w

def kernel(n_r, n_c, n_cc, nb, x_ref, o_ref, work, diag, fbuf, panels,
           f_send, f_recv, row_send, col_send, p_recv):
    parts = nb // BLK
    r = lax.axis_index("pr")
    c = lax.axis_index("pc")
    near = lax.rem(c + 1, n_c)

    barrier = pltpu.get_barrier_semaphore()

    def greet(i, _):
        @pl.when(i != r * n_c + c)
        def _():
            pl.semaphore_signal(
                barrier, inc=1, device_id={"pr": i // n_c, "pc": lax.rem(i, n_c)},
                device_id_type=pl.DeviceIdType.MESH)
        return 0

    lax.fori_loop(0, n_r * n_c, greet, 0)
    o_ref[...] = x_ref[...]

    i0 = lax.broadcasted_iota(jnp.int32, (BLK, BLK), 0)
    i1 = lax.broadcasted_iota(jnp.int32, (BLK, BLK), 1)

    @pl.when(c < 2)
    def _():
        for m in range(parts):
            work[m] = x_ref[0, :, m * BLK:(m + 1) * BLK]

        @pl.when(r == c)
        def _():
            for m in range(parts):
                block = work[m, m * BLK:(m + 1) * BLK, :]
                work[m, m * BLK:(m + 1) * BLK, :] = jnp.where(i0 >= i1, block, block.T)

    pl.semaphore_wait(barrier, n_r * n_c - 1)

    def factor_copy(k, m):
        ref = fbuf.at[k, m, pl.ds(m * BLK, nb - m * BLK), :]
        return pltpu.make_async_remote_copy(
            src_ref=ref, dst_ref=ref, send_sem=f_send.at[k, m], recv_sem=f_recv.at[k, m],
            device_id={"pr": lax.rem(r + 1, n_r)}, device_id_type=pl.DeviceIdType.MESH)

    def row_copy(k, m, to):
        ref = panels.at[k, 0, m]
        return pltpu.make_async_remote_copy(
            src_ref=ref, dst_ref=ref, send_sem=row_send.at[k, m, to], recv_sem=p_recv.at[k, 0, m],
            device_id={"pc": to}, device_id_type=pl.DeviceIdType.MESH)

    def col_copy(k, m, source, slot, to_c):
        return pltpu.make_async_remote_copy(
            src_ref=panels.at[k, source, m], dst_ref=panels.at[k, slot, m],
            send_sem=col_send.at[k, source, m], recv_sem=p_recv.at[k, slot, m],
            device_id={"pr": lax.rem(r + 1, n_r), "pc": to_c},
            device_id_type=pl.DeviceIdType.MESH)

    def holds(k, row, col):
        found = (col > k) & (col <= row)
        for b in range(1, n_cc):
            found = found | ((b * n_c + col > k) & (b * n_c + col <= row))
        return found

    def each_row_copy(k, m, act):
        for to in range(n_c):
            pair = (k // 2) * 2
            first = (to == pair + 1 - (k - pair)) | ((to % 2 == 0) & (to != pair))

            @pl.when(first & holds(k, r, to))
            def _():
                act(row_copy(k, m, to))

    def hand_on_row(k, m, act):
        @pl.when((c % 2 == 0) & (c // 2 != k // 2) & holds(k, r, c + 1))
        def _():
            act(row_copy(k, m, lax.rem(c + 1, n_c)))

    def own_col_copy(k, m, act):
        @pl.when(r + 1 < n_r)
        def _():
            act(col_copy(k, m, 0, 1 + r // n_c, lax.rem(r, n_c)))

    def hand_on_col(k, m, b, act):
        @pl.when(r + 1 < n_r)
        def _():
            act(col_copy(k, m, 1 + b, 1 + b, c))

    def hand_on_factor(k, m, act):
        @pl.when(r + 1 < n_r)
        def _():
            act(factor_copy(k, m))

    start = lambda d: d.start()
    sent = lambda d: d.wait_send()

    def step(k, _):
        is_factor = (r == k) & (c == k)
        is_solver = (c == k) & (r > k)

        @pl.when(is_factor)
        def _():
            a = work[0, :BLK, :]
            for m in range(parts):
                s, e = m * BLK, (m + 1) * BLK
                lt, w = factor_block(a)
                diag[m] = lt
                fbuf[k, m, s:e, :] = w
                if m + 1 < parts:
                    f = e + BLK
                    head = nt(work[m, e:f, :], w)
                    a = work[m + 1, e:f, :] - nt(head, head)
                    fbuf[k, m, e:f, :] = head
                    if f < nb:
                        fbuf[k, m, f:, :] = nt(work[m, f:, :], w)
                factor_copy(k, m).start()
                if m + 2 < parts:
                    work[m + 1, f:, :] -= nt(fbuf[k, m, f:, :], head)
                for n in range(m + 2, parts):
                    t = n * BLK
                    work[n, t:, :] -= nt(fbuf[k, m, t:, :], fbuf[k, m, t:t + BLK, :])
            for m in range(parts):
                s, e = m * BLK, (m + 1) * BLK
                if m:
                    o_ref[0, :s, s:e] = jnp.zeros((s, BLK), jnp.float32)
                o_ref[0, s:e, s:e] = jnp.where(i0 <= i1, diag[m], 0.0).T
                if e < nb:
                    o_ref[0, e:, s:e] = fbuf[k, m, e:, :]
            for m in range(parts):
                factor_copy(k, m).wait_send()

        @pl.when(is_solver)
        def _():
            for m in range(parts):
                s, e = m * BLK, (m + 1) * BLK
                factor_copy(k, m).wait_recv()
                hand_on_factor(k, m, start)
                part = nt(work[m], fbuf[k, m, s:e, :])
                panels[k, 0, m] = part
                each_row_copy(k, m, start)
                own_col_copy(k, m, start)
                o_ref[0, :, s:e] = part
                for n in range(m + 1, parts):
                    work[n] -= nt(part, fbuf[k, m, n * BLK:(n + 1) * BLK, :])

        for m in range(parts):
            @pl.when((c != k) & holds(k, r, c))
            def _():
                row_copy(k, m, near).wait_recv()
                hand_on_row(k, m, start)
            for b in range(n_cc):
                j = b * n_c + c
                active = (j > k) & (j <= r)
                kept = (k == 0) & (c == 1) if b == 0 else False

                @pl.when((j > k) & (j < r))
                def _():
                    col_copy(k, m, 1 + b, 1 + b, c).wait_recv()
                    hand_on_col(k, m, b, start)

                if b == 0:
                    @pl.when(active & kept & (r == 1))
                    def _():
                        for n in range(parts):
                            t = n * BLK
                            work[n, t:, :] -= nt(panels[k, 0, m, t:, :], panels[k, 0, m, t:t + BLK, :])

                    @pl.when(active & kept & (r > 1))
                    def _():
                        for n in range(parts):
                            work[n] -= nt(panels[k, 0, m], panels[k, 1, m, n * BLK:(n + 1) * BLK, :])

                @pl.when(active & jnp.logical_not(kept))
                def _():
                    slot = jnp.where(j == r, 0, 1 + b)
                    o_ref[b] -= nt(panels[k, 0, m], panels[k, slot, m])

        for m in range(parts):
            @pl.when(is_solver)
            def _():
                hand_on_factor(k, m, sent)
                each_row_copy(k, m, sent)
                own_col_copy(k, m, sent)

            @pl.when((c != k) & holds(k, r, c))
            def _():
                hand_on_row(k, m, sent)
            for b in range(n_cc):
                j = b * n_c + c

                @pl.when((j > k) & (j < r))
                def _():
                    hand_on_col(k, m, b, sent)
        return 0

    lax.fori_loop(0, 2, step, 0)


def on_device(n_r, n_c, matrix):
    _, nb, n_cc, _ = matrix.shape
    parts = nb // BLK
    tiles = jnp.transpose(matrix[0], (1, 0, 2))
    sem = pltpu.SemaphoreType.DMA
    out = pl.pallas_call(
        functools.partial(kernel, n_r, n_c, n_cc, nb),
        out_shape=jax.ShapeDtypeStruct(tiles.shape, jnp.float32),
        in_specs=[pl.BlockSpec(memory_space=pltpu.VMEM)],
        out_specs=pl.BlockSpec(memory_space=pltpu.VMEM),
        scratch_shapes=[
            pltpu.VMEM((parts, nb, BLK), jnp.float32),
            pltpu.VMEM((parts, BLK, BLK), jnp.float32),
            pltpu.VMEM((2, parts, nb, BLK), jnp.float32),
            pltpu.VMEM((2, 1 + n_cc, parts, nb, BLK), jnp.float32),
            sem((2, parts)),
            sem((2, parts)),
            sem((2, parts, n_c)),
            sem((2, 1 + n_cc, parts)),
            sem((2, 1 + n_cc, parts)),
        ],
        compiler_params=pltpu.CompilerParams(
            collective_id=0, has_side_effects=True, vmem_limit_bytes=40 * 2**20),
    )(tiles)
    return jnp.transpose(out, (1, 0, 2))[None]


def solution(mesh):
    n_r, n_c = mesh.shape["pr"], mesh.shape["pc"]
    spec = P("groups", "pr", None, "pc")
    return jax.shard_map(
        functools.partial(on_device, n_r, n_c), mesh=mesh, in_specs=(spec,), out_specs=spec,
        check_vma=False)
```

```python
import functools

import jax
import jax.numpy as jnp
from jax import lax
from jax.experimental import pallas as pl
from jax.experimental.pallas import tpu as pltpu
from jax.sharding import PartitionSpec as P

BLK = 128
G = 8
SUPER = 8


def nt(a, b):
    return lax.dot_general(
        a, b, (((1,), (1,)), ((), ())),
        precision=lax.Precision.HIGHEST, preferred_element_type=jnp.float32,
    )


def factor_block(a):
    n = BLK
    ng = n // G
    sub = lax.broadcasted_iota(jnp.int32, (G, n), 0)
    lane = lax.broadcasted_iota(jnp.int32, (G, n), 1)
    left = [a[g * G:(g + 1) * G, :] for g in range(ng)]
    right = [jnp.where(lane == sub + g * G, 1.0, 0.0).astype(jnp.float32) for g in range(ng)]
    for s0 in range(0, ng, SUPER):
        s1 = min(s0 + SUPER, ng)
        for g in range(s0, s1):
            own_l, own_r = left[g], right[g]
            lo = g * G
            later = range(g + 1, s1)
            own_c = [jnp.broadcast_to(own_l[:, lo + j:lo + j + 1], (G, n)) for j in range(G)]
            cols = {h: [jnp.broadcast_to(left[h][:, lo + j:lo + j + 1], (G, n)) for j in range(G)]
                    for h in later}
            rows_l, rows_r = [], []
            for j in range(G):
                q = lax.rsqrt(jnp.broadcast_to(own_c[j][j:j + 1, :], (G, n)))
                row_l = jnp.broadcast_to(own_l[j:j + 1, :], (G, n)) * q
                row_r = jnp.broadcast_to(own_r[j:j + 1, :], (G, n)) * q
                rows_l.append(row_l)
                rows_r.append(row_r)
                mult = own_c[j] * q
                heads = [jnp.broadcast_to(own_c[t][j:j + 1, :], (G, n)) * q for t in range(j + 1, G)]
                for t in range(j + 1, G):
                    own_c[t] = own_c[t] - mult * heads[t - j - 1]
                own_l = own_l - mult * row_l
                own_r = own_r - mult * row_r
                for h in later:
                    c = cols[h]
                    mult = c[j] * q
                    for t in range(j + 1, G):
                        c[t] = c[t] - mult * heads[t - j - 1]
                    left[h] = left[h] - mult * row_l
                    right[h] = right[h] - mult * row_r
            fin_l, fin_r = rows_l[0], rows_r[0]
            for j in range(1, G):
                fin_l = jnp.where(sub == j, rows_l[j], fin_l)
                fin_r = jnp.where(sub == j, rows_r[j], fin_r)
            left[g], right[g] = fin_l, fin_r
        if s1 < ng:
            top = jnp.concatenate(left[s0:s1], 0)
            both = jnp.concatenate([top, jnp.concatenate(right[s0:s1], 0)], 1)
            prod = lax.dot_general(top[:, s1 * G:], both, (((0,), (0,)), ((), ())),
                                   precision=lax.Precision.HIGHEST,
                                   preferred_element_type=jnp.float32)
            for h in range(s1, ng):
                o = (h - s1) * G
                left[h] = left[h] - prod[o:o + G, :n]
                right[h] = right[h] - prod[o:o + G, n:]
    lt = jnp.concatenate(left, 0)
    w = jnp.concatenate(right, 0)
    return lt, w

def kernel(n_r, n_c, n_cc, nb, x_ref, o_ref, work, diag, fbuf, panels,
           f_send, f_recv, row_send, col_send, p_recv):
    parts = nb // BLK
    r = lax.axis_index("pr")
    c = lax.axis_index("pc")
    near = lax.rem(c + 1, n_c)

    barrier = pltpu.get_barrier_semaphore()

    def greet(i, _):
        @pl.when(i != r * n_c + c)
        def _():
            pl.semaphore_signal(
                barrier, inc=1, device_id={"pr": i // n_c, "pc": lax.rem(i, n_c)},
                device_id_type=pl.DeviceIdType.MESH)
        return 0

    lax.fori_loop(0, n_r * n_c, greet, 0)
    o_ref[...] = x_ref[...]

    i0 = lax.broadcasted_iota(jnp.int32, (BLK, BLK), 0)
    i1 = lax.broadcasted_iota(jnp.int32, (BLK, BLK), 1)

    @pl.when(c < 2)
    def _():
        for m in range(parts):
            work[m] = x_ref[0, :, m * BLK:(m + 1) * BLK]

        @pl.when(r == c)
        def _():
            for m in range(parts):
                block = work[m, m * BLK:(m + 1) * BLK, :]
                work[m, m * BLK:(m + 1) * BLK, :] = jnp.where(i0 >= i1, block, block.T)

    pl.semaphore_wait(barrier, n_r * n_c - 1)

    def factor_copy(k, m):
        ref = fbuf.at[k, m, pl.ds(m * BLK, nb - m * BLK), :]
        return pltpu.make_async_remote_copy(
            src_ref=ref, dst_ref=ref, send_sem=f_send.at[k, m], recv_sem=f_recv.at[k, m],
            device_id={"pr": lax.rem(r + 1, n_r)}, device_id_type=pl.DeviceIdType.MESH)

    def row_copy(k, m, to):
        ref = panels.at[k, 0, m]
        return pltpu.make_async_remote_copy(
            src_ref=ref, dst_ref=ref, send_sem=row_send.at[k, m, to], recv_sem=p_recv.at[k, 0, m],
            device_id={"pc": to}, device_id_type=pl.DeviceIdType.MESH)

    def col_copy(k, m, source, slot, to_c):
        return pltpu.make_async_remote_copy(
            src_ref=panels.at[k, source, m], dst_ref=panels.at[k, slot, m],
            send_sem=col_send.at[k, source, m], recv_sem=p_recv.at[k, slot, m],
            device_id={"pr": lax.rem(r + 1, n_r), "pc": to_c},
            device_id_type=pl.DeviceIdType.MESH)

    def holds(k, row, col):
        found = (col > k) & (col <= row)
        for b in range(1, n_cc):
            found = found | ((b * n_c + col > k) & (b * n_c + col <= row))
        return found

    def each_row_copy(k, m, act):
        for to in range(n_c):
            pair = (k // 2) * 2
            first = (to == pair + 1 - (k - pair)) | ((to % 2 == 0) & (to != pair))

            @pl.when(first & holds(k, r, to))
            def _():
                act(row_copy(k, m, to))

    def hand_on_row(k, m, act):
        @pl.when((c % 2 == 0) & (c // 2 != k // 2) & holds(k, r, c + 1))
        def _():
            act(row_copy(k, m, lax.rem(c + 1, n_c)))

    def own_col_copy(k, m, b, act):
        @pl.when(r + 1 < n_r)
        def _():
            act(col_copy(k, m, 0, 1 + b, c))

    def hand_on_col(k, m, b, act):
        @pl.when(r + 1 < n_r)
        def _():
            act(col_copy(k, m, 1 + b, 1 + b, c))

    def hand_on_factor(k, m, act):
        @pl.when(r + 1 < n_r)
        def _():
            act(factor_copy(k, m))

    start = lambda d: d.start()
    sent = lambda d: d.wait_send()

    def step(k, _):
        is_factor = (r == k) & (c == k)
        is_solver = (c == k) & (r > k)

        @pl.when(is_factor)
        def _():
            a = work[0, :BLK, :]
            for m in range(parts):
                s, e = m * BLK, (m + 1) * BLK
                lt, w = factor_block(a)
                diag[m] = lt
                fbuf[k, m, s:e, :] = w
                if m + 1 < parts:
                    f = e + BLK
                    head = nt(work[m, e:f, :], w)
                    a = work[m + 1, e:f, :] - nt(head, head)
                    fbuf[k, m, e:f, :] = head
                    if f < nb:
                        fbuf[k, m, f:, :] = nt(work[m, f:, :], w)
                factor_copy(k, m).start()
                if m + 2 < parts:
                    work[m + 1, f:, :] -= nt(fbuf[k, m, f:, :], head)
                for n in range(m + 2, parts):
                    t = n * BLK
                    work[n, t:, :] -= nt(fbuf[k, m, t:, :], fbuf[k, m, t:t + BLK, :])
            for m in range(parts):
                s, e = m * BLK, (m + 1) * BLK
                if m:
                    o_ref[0, :s, s:e] = jnp.zeros((s, BLK), jnp.float32)
                o_ref[0, s:e, s:e] = jnp.where(i0 <= i1, diag[m], 0.0).T
                if e < nb:
                    o_ref[0, e:, s:e] = fbuf[k, m, e:, :]
            for m in range(parts):
                factor_copy(k, m).wait_send()

        @pl.when(is_solver)
        def _():
            for m in range(parts):
                s, e = m * BLK, (m + 1) * BLK
                factor_copy(k, m).wait_recv()
                hand_on_factor(k, m, start)
                part = nt(work[m], fbuf[k, m, s:e, :])
                panels[k, 0, m] = part
                each_row_copy(k, m, start)
                o_ref[0, :, s:e] = part
                for n in range(m + 1, parts):
                    work[n] -= nt(part, fbuf[k, m, n * BLK:(n + 1) * BLK, :])

        for m in range(parts):
            @pl.when((c != k) & holds(k, r, c))
            def _():
                row_copy(k, m, near).wait_recv()
                hand_on_row(k, m, start)
            for b in range(n_cc):
                j = b * n_c + c
                active = (j > k) & (j <= r)
                kept = (k == 0) & (c == 1) if b == 0 else False

                @pl.when((j > k) & (j < r))
                def _():
                    col_copy(k, m, 1 + b, 1 + b, c).wait_recv()
                    hand_on_col(k, m, b, start)

                @pl.when((j > k) & (j == r))
                def _():
                    own_col_copy(k, m, b, start)

                if b == 0:
                    @pl.when(active & kept & (r == 1))
                    def _():
                        for n in range(parts):
                            t = n * BLK
                            work[n, t:, :] -= nt(panels[k, 0, m, t:, :], panels[k, 0, m, t:t + BLK, :])

                    @pl.when(active & kept & (r > 1))
                    def _():
                        for n in range(parts):
                            work[n] -= nt(panels[k, 0, m], panels[k, 1, m, n * BLK:(n + 1) * BLK, :])

                @pl.when(active & jnp.logical_not(kept))
                def _():
                    slot = jnp.where(j == r, 0, 1 + b)
                    o_ref[b] -= nt(panels[k, 0, m], panels[k, slot, m])

        for m in range(parts):
            @pl.when(is_solver)
            def _():
                hand_on_factor(k, m, sent)
                each_row_copy(k, m, sent)

            @pl.when((c != k) & holds(k, r, c))
            def _():
                hand_on_row(k, m, sent)
            for b in range(n_cc):
                j = b * n_c + c

                @pl.when((j > k) & (j < r))
                def _():
                    hand_on_col(k, m, b, sent)

                @pl.when((j > k) & (j == r))
                def _():
                    own_col_copy(k, m, b, sent)
        return 0

    lax.fori_loop(0, 2, step, 0)


def on_device(n_r, n_c, matrix):
    _, nb, n_cc, _ = matrix.shape
    parts = nb // BLK
    tiles = jnp.transpose(matrix[0], (1, 0, 2))
    sem = pltpu.SemaphoreType.DMA
    out = pl.pallas_call(
        functools.partial(kernel, n_r, n_c, n_cc, nb),
        out_shape=jax.ShapeDtypeStruct(tiles.shape, jnp.float32),
        in_specs=[pl.BlockSpec(memory_space=pltpu.VMEM)],
        out_specs=pl.BlockSpec(memory_space=pltpu.VMEM),
        scratch_shapes=[
            pltpu.VMEM((parts, nb, BLK), jnp.float32),
            pltpu.VMEM((parts, BLK, BLK), jnp.float32),
            pltpu.VMEM((2, parts, nb, BLK), jnp.float32),
            pltpu.VMEM((2, 1 + n_cc, parts, nb, BLK), jnp.float32),
            sem((2, parts)),
            sem((2, parts)),
            sem((2, parts, n_c)),
            sem((2, 1 + n_cc, parts)),
            sem((2, 1 + n_cc, parts)),
        ],
        compiler_params=pltpu.CompilerParams(
            collective_id=0, has_side_effects=True, vmem_limit_bytes=40 * 2**20),
    )(tiles)
    return jnp.transpose(out, (1, 0, 2))[None]


def solution(mesh):
    n_r, n_c = mesh.shape["pr"], mesh.shape["pc"]
    spec = P("groups", "pr", None, "pc")
    return jax.shard_map(
        functools.partial(on_device, n_r, n_c), mesh=mesh, in_specs=(spec,), out_specs=spec,
        check_vma=False)
```

```python
import functools

import jax
import jax.numpy as jnp
from jax import lax
from jax.experimental import pallas as pl
from jax.experimental.pallas import tpu as pltpu
from jax.sharding import PartitionSpec as P

BLK = 128
G = 8
SUPER = 8


def nt(a, b):
    return lax.dot_general(
        a, b, (((1,), (1,)), ((), ())),
        precision=lax.Precision.HIGHEST, preferred_element_type=jnp.float32,
    )


def factor_block(a, jobs=()):
    n = BLK
    ng = n // G
    sub = lax.broadcasted_iota(jnp.int32, (G, n), 0)
    lane = lax.broadcasted_iota(jnp.int32, (G, n), 1)
    left = [a[g * G:(g + 1) * G, :] for g in range(ng)]
    right = [jnp.where(lane == sub + g * G, 1.0, 0.0).astype(jnp.float32) for g in range(ng)]
    for s0 in range(0, ng, SUPER):
        s1 = min(s0 + SUPER, ng)
        for g in range(s0, s1):
            own_l, own_r = left[g], right[g]
            lo = g * G
            later = range(g + 1, s1)
            own_c = [jnp.broadcast_to(own_l[:, lo + j:lo + j + 1], (G, n)) for j in range(G)]
            cols = {h: [jnp.broadcast_to(left[h][:, lo + j:lo + j + 1], (G, n)) for j in range(G)]
                    for h in later}
            rows_l, rows_r = [], []
            for j in range(G):
                q = lax.rsqrt(jnp.broadcast_to(own_c[j][j:j + 1, :], (G, n)))
                row_l = jnp.broadcast_to(own_l[j:j + 1, :], (G, n)) * q
                row_r = jnp.broadcast_to(own_r[j:j + 1, :], (G, n)) * q
                rows_l.append(row_l)
                rows_r.append(row_r)
                mult = own_c[j] * q
                heads = [jnp.broadcast_to(own_c[t][j:j + 1, :], (G, n)) * q for t in range(j + 1, G)]
                for t in range(j + 1, G):
                    own_c[t] = own_c[t] - mult * heads[t - j - 1]
                own_l = own_l - mult * row_l
                own_r = own_r - mult * row_r
                for h in later:
                    c = cols[h]
                    mult = c[j] * q
                    for t in range(j + 1, G):
                        c[t] = c[t] - mult * heads[t - j - 1]
                    left[h] = left[h] - mult * row_l
                    right[h] = right[h] - mult * row_r
            fin_l, fin_r = rows_l[0], rows_r[0]
            for j in range(1, G):
                fin_l = jnp.where(sub == j, rows_l[j], fin_l)
                fin_r = jnp.where(sub == j, rows_r[j], fin_r)
            left[g], right[g] = fin_l, fin_r
            if g < len(jobs):
                jobs[g]()
        if s1 < ng:
            top = jnp.concatenate(left[s0:s1], 0)
            both = jnp.concatenate([top, jnp.concatenate(right[s0:s1], 0)], 1)
            prod = lax.dot_general(top[:, s1 * G:], both, (((0,), (0,)), ((), ())),
                                   precision=lax.Precision.HIGHEST,
                                   preferred_element_type=jnp.float32)
            for h in range(s1, ng):
                o = (h - s1) * G
                left[h] = left[h] - prod[o:o + G, :n]
                right[h] = right[h] - prod[o:o + G, n:]
    lt = jnp.concatenate(left, 0)
    w = jnp.concatenate(right, 0)
    return lt, w

def kernel(n_r, n_c, n_cc, nb, x_ref, o_ref, work, diag, fbuf, panels,
           f_send, f_recv, row_send, col_send, p_recv):
    parts = nb // BLK
    r = lax.axis_index("pr")
    c = lax.axis_index("pc")
    near = lax.rem(c + 1, n_c)

    barrier = pltpu.get_barrier_semaphore()

    def greet(i, _):
        @pl.when(i != r * n_c + c)
        def _():
            pl.semaphore_signal(
                barrier, inc=1, device_id={"pr": i // n_c, "pc": lax.rem(i, n_c)},
                device_id_type=pl.DeviceIdType.MESH)
        return 0

    lax.fori_loop(0, n_r * n_c, greet, 0)

    @pl.when((c >= 2) | (r < c))
    def _():
        o_ref[0] = x_ref[0]

    for b in range(1, n_cc):
        o_ref[b] = x_ref[b]


    i0 = lax.broadcasted_iota(jnp.int32, (BLK, BLK), 0)
    i1 = lax.broadcasted_iota(jnp.int32, (BLK, BLK), 1)

    @pl.when(c < 2)
    def _():
        for m in range(parts):
            work[m] = x_ref[0, :, m * BLK:(m + 1) * BLK]

        @pl.when(r == c)
        def _():
            for m in range(parts):
                block = work[m, m * BLK:(m + 1) * BLK, :]
                work[m, m * BLK:(m + 1) * BLK, :] = jnp.where(i0 >= i1, block, block.T)

    @pl.when((r != 0) | (c != 0))
    def _():
        pl.semaphore_wait(barrier, n_r * n_c - 1)

    def factor_copy(k, m):
        ref = fbuf.at[k, m, pl.ds(m * BLK, nb - m * BLK), :]
        return pltpu.make_async_remote_copy(
            src_ref=ref, dst_ref=ref, send_sem=f_send.at[k, m], recv_sem=f_recv.at[k, m],
            device_id={"pr": lax.rem(r + 1, n_r)}, device_id_type=pl.DeviceIdType.MESH)

    def row_copy(k, m, to):
        ref = panels.at[k, 0, m]
        return pltpu.make_async_remote_copy(
            src_ref=ref, dst_ref=ref, send_sem=row_send.at[k, m, to], recv_sem=p_recv.at[k, 0, m],
            device_id={"pc": to}, device_id_type=pl.DeviceIdType.MESH)

    def col_copy(k, m, source, slot, to_c):
        return pltpu.make_async_remote_copy(
            src_ref=panels.at[k, source, m], dst_ref=panels.at[k, slot, m],
            send_sem=col_send.at[k, source, m], recv_sem=p_recv.at[k, slot, m],
            device_id={"pr": lax.rem(r + 1, n_r), "pc": to_c},
            device_id_type=pl.DeviceIdType.MESH)

    def holds(k, row, col):
        found = (col > k) & (col <= row)
        for b in range(1, n_cc):
            found = found | ((b * n_c + col > k) & (b * n_c + col <= row))
        return found

    def each_row_copy(k, m, act):
        for to in range(n_c):
            pair = (k // 2) * 2
            first = (to == pair + 1 - (k - pair)) | ((to % 2 == 0) & (to != pair))

            @pl.when(first & holds(k, r, to))
            def _():
                act(row_copy(k, m, to))

    def hand_on_row(k, m, act):
        @pl.when((c % 2 == 0) & (c // 2 != k // 2) & holds(k, r, c + 1))
        def _():
            act(row_copy(k, m, lax.rem(c + 1, n_c)))

    def own_col_copy(k, m, b, act):
        @pl.when(r + 1 < n_r)
        def _():
            act(col_copy(k, m, 0, 1 + b, c))

    def hand_on_col(k, m, b, act):
        @pl.when(r + 1 < n_r)
        def _():
            act(col_copy(k, m, 1 + b, 1 + b, c))

    def hand_on_factor(k, m, act):
        @pl.when(r + 1 < n_r)
        def _():
            act(factor_copy(k, m))

    start = lambda d: d.start()
    sent = lambda d: d.wait_send()

    def step(k, _):
        is_factor = (r == k) & (c == k)
        is_solver = (c == k) & (r > k)

        @pl.when(is_factor)
        def _():
            a = work[0, :BLK, :]
            jobs = []
            for m in range(parts):
                s, e = m * BLK, (m + 1) * BLK
                lt, w = factor_block(a, jobs)
                diag[m] = lt
                fbuf[k, m, s:e, :] = w
                if m == 0:
                    @pl.when(k == 0)
                    def _():
                        pl.semaphore_wait(barrier, n_r * n_c - 1)
                if m + 1 == parts:
                    factor_copy(k, m).start()
                    break
                f = e + BLK
                head = nt(work[m, e:f, :], w)
                a = work[m + 1, e:f, :] - nt(head, head)
                fbuf[k, m, e:f, :] = head

                def finish(m=m, f=f, w=w):
                    if f < nb:
                        fbuf[k, m, f:, :] = nt(work[m, f:, :], w)
                    factor_copy(k, m).start()

                def trail(n, m=m, e=e):
                    t = max(n * BLK, e + BLK)
                    work[n, t:, :] -= nt(fbuf[k, m, t:, :], fbuf[k, m, n * BLK:(n + 1) * BLK, :])

                jobs = [finish]
                for n in range(m + 1, parts):
                    if max(n * BLK, f) < nb:
                        jobs.append(functools.partial(trail, n))
            for m in range(parts):
                s, e = m * BLK, (m + 1) * BLK
                if m:
                    o_ref[0, :s, s:e] = jnp.zeros((s, BLK), jnp.float32)
                o_ref[0, s:e, s:e] = jnp.where(i0 <= i1, diag[m], 0.0).T
                if e < nb:
                    o_ref[0, e:, s:e] = fbuf[k, m, e:, :]
            for m in range(parts):
                factor_copy(k, m).wait_send()

        @pl.when(is_solver)
        def _():
            for m in range(parts):
                s, e = m * BLK, (m + 1) * BLK
                factor_copy(k, m).wait_recv()
                hand_on_factor(k, m, start)
                part = nt(work[m], fbuf[k, m, s:e, :])
                panels[k, 0, m] = part
                each_row_copy(k, m, start)
                o_ref[0, :, s:e] = part
                for n in range(m + 1, parts):
                    work[n] -= nt(part, fbuf[k, m, n * BLK:(n + 1) * BLK, :])

        for m in range(parts):
            @pl.when((c != k) & holds(k, r, c))
            def _():
                row_copy(k, m, near).wait_recv()
                hand_on_row(k, m, start)
            for b in range(n_cc):
                j = b * n_c + c
                active = (j > k) & (j <= r)
                kept = (k == 0) & (c == 1) if b == 0 else False

                @pl.when((j > k) & (j < r))
                def _():
                    col_copy(k, m, 1 + b, 1 + b, c).wait_recv()
                    hand_on_col(k, m, b, start)

                @pl.when((j > k) & (j == r))
                def _():
                    own_col_copy(k, m, b, start)

                if b == 0:
                    @pl.when(active & kept & (r == 1))
                    def _():
                        for n in range(parts):
                            t = n * BLK
                            work[n, t:, :] -= nt(panels[k, 0, m, t:, :], panels[k, 0, m, t:t + BLK, :])

                    @pl.when(active & kept & (r > 1))
                    def _():
                        for n in range(parts):
                            work[n] -= nt(panels[k, 0, m], panels[k, 1, m, n * BLK:(n + 1) * BLK, :])

                @pl.when(active & jnp.logical_not(kept))
                def _():
                    slot = jnp.where(j == r, 0, 1 + b)
                    o_ref[b] -= nt(panels[k, 0, m], panels[k, slot, m])

        for m in range(parts):
            @pl.when(is_solver)
            def _():
                hand_on_factor(k, m, sent)
                each_row_copy(k, m, sent)

            @pl.when((c != k) & holds(k, r, c))
            def _():
                hand_on_row(k, m, sent)
            for b in range(n_cc):
                j = b * n_c + c

                @pl.when((j > k) & (j < r))
                def _():
                    hand_on_col(k, m, b, sent)

                @pl.when((j > k) & (j == r))
                def _():
                    own_col_copy(k, m, b, sent)
        return 0

    lax.fori_loop(0, 2, step, 0)


def on_device(n_r, n_c, matrix):
    _, nb, n_cc, _ = matrix.shape
    parts = nb // BLK
    tiles = jnp.transpose(matrix[0], (1, 0, 2))
    sem = pltpu.SemaphoreType.DMA
    out = pl.pallas_call(
        functools.partial(kernel, n_r, n_c, n_cc, nb),
        out_shape=jax.ShapeDtypeStruct(tiles.shape, jnp.float32),
        in_specs=[pl.BlockSpec(memory_space=pltpu.VMEM)],
        out_specs=pl.BlockSpec(memory_space=pltpu.VMEM),
        scratch_shapes=[
            pltpu.VMEM((parts, nb, BLK), jnp.float32),
            pltpu.VMEM((parts, BLK, BLK), jnp.float32),
            pltpu.VMEM((2, parts, nb, BLK), jnp.float32),
            pltpu.VMEM((2, 1 + n_cc, parts, nb, BLK), jnp.float32),
            sem((2, parts)),
            sem((2, parts)),
            sem((2, parts, n_c)),
            sem((2, 1 + n_cc, parts)),
            sem((2, 1 + n_cc, parts)),
        ],
        compiler_params=pltpu.CompilerParams(
            collective_id=0, has_side_effects=True, vmem_limit_bytes=40 * 2**20),
    )(tiles)
    return jnp.transpose(out, (1, 0, 2))[None]


def solution(mesh):
    n_r, n_c = mesh.shape["pr"], mesh.shape["pc"]
    spec = P("groups", "pr", None, "pc")
    return jax.shard_map(
        functools.partial(on_device, n_r, n_c), mesh=mesh, in_specs=(spec,), out_specs=spec,
        check_vma=False)
```
